32 devices in a mesh: tok: 4 (over y, core), wt: 8 (over z, x).
Axes of the slice: x: 2, y: 2, z: 4, core: 2. Of those that a mesh axis runs over, the one named last changes fastest.
Arguments:
- activations: bfloat16 [1536, 8192], P('tok', 'wt'), may hold values from -6 to 6
- gate_pre: bfloat16 [1536, 16384], P('tok', 'wt'), may hold values from -6 to 6
- up_pre: bfloat16 [1536, 16384], P('tok', 'wt'), may hold values from -6 to 6
- hidden_grad: bfloat16 [1536, 16384], P('tok', 'wt'), may hold values from -0.59765625 to 0.59765625
- gate_blocks: bfloat16 [4096, 128, 128], P('wt'), may hold values from -0.125 to 0.125
- up_blocks: bfloat16 [4096, 128, 128], P('wt'), may hold values from -0.125 to 0.125
- block_rows: int32 [4096], P('wt'), may hold values from 0 to 127, as said below
- block_cols: int32 [4096], P('wt'), may hold values from 0 to 63, as said below
- block_count: int32 [8], P('wt'), may hold values from 128 to 512, as said below
Outputs:
- input_grad: bfloat16 [1536, 8192], P('tok', 'wt')
- gate_weight_grad: bfloat16 [4096, 128, 128], P('wt')
- up_weight_grad: bfloat16 [4096, 128, 128], P('wt')
The draws below stay inside these ranges and needn't reach their ends.
Inputs may be any that keep to these rules, and one draw needn't show every extreme that they name: `block_rows`: slots of wt index w are w * 512 to (w + 1) * 512 - 1; their block rows lie in w * 16 to (w + 1) * 16 - 1; slots past the count repeat the owner's first slot. `block_cols`: the live slots of one owner name distinct blocks. `block_count`: one owner holds exactly 512 kept blocks.
All inputs are finite; a program needn't handle non-finite values.
Results may differ from the reference program's by a relative error of at most 0.025.
Values may be sent and summed in bfloat16 or wider, within the bound.
A program may use at most 320 MiB of HBM per device.

```python
import jax
import jax.numpy as jnp
from jax import lax

D = 8192
FF = 16384
BLK = 128
TOK_DEV = 384
TOKENS = 1536
DBLK = 64
FBLK = 128
ROWS_DEV = 16
KEEP = 256
MAXB = 512
N_TOK = 4
N_WT = 8


def pattern(key):
    counts = jax.random.randint(jax.random.fold_in(key, 1), (N_WT,), KEEP // 2, 3 * KEEP // 2 + 1)
    heavy = jax.random.randint(jax.random.fold_in(key, 2), (), 0, N_WT)
    counts = jnp.where(jnp.arange(N_WT) == heavy, MAXB, counts).astype(jnp.int32)
    pairs = ROWS_DEV * DBLK
    scores = jax.random.randint(jax.random.fold_in(key, 3), (N_WT, pairs), 0, 1024) * pairs + jnp.arange(pairs)[None, :]
    order = jnp.argsort(scores, axis=1)[:, :MAXB]
    slot_index = jnp.arange(MAXB)[None, :]
    chosen = jnp.where(slot_index < counts[:, None], order, order[:, :1])
    rows = jnp.arange(N_WT)[:, None] * ROWS_DEV + chosen // DBLK
    cols = chosen % DBLK
    return (counts, rows.reshape(-1).astype(jnp.int32), cols.reshape(-1).astype(jnp.int32))


def draw_block_rows(key, part):
    shared = pattern(key)
    return shared[1]


def draw_block_cols(key, part):
    shared = pattern(key)
    return shared[2]


def draw_block_count(key, part):
    shared = pattern(key)
    return shared[0]


def shard_levels(own_key, shape, cuts, least, high):
    def one(position, parts):
        steps = jax.random.uniform(jax.random.fold_in(jax.random.fold_in(own_key, 6), position), (parts,), jnp.float32, least / len(cuts), high / len(cuts))
        return jnp.repeat(jnp.exp(steps), shape[position] // parts).reshape((-1,) + (1,) * (len(shape) - position - 1))

    gain = one(*cuts[0])
    for cut in cuts[1:]:
        gain = gain * one(*cut)
    return gain


def gaussian(key, dims, deviation, reach, split=(), kind=jnp.bfloat16):
    entries = deviation * jax.random.normal(key, dims, jnp.float32)
    if split:
        entries = entries * shard_levels(key, dims, split, -0.22, 0.18)
    return jnp.clip(entries, -reach, reach).astype(kind)


def setup_inputs(seed: int = 0) -> dict:
    arg_keys = jax.random.split(jax.random.key(seed), 10)
    activations = gaussian(arg_keys[0], (TOKENS, D), 1.0, 6.0, ((0, 4), (1, 8)))
    gate_pre = gaussian(arg_keys[1], (TOKENS, FF), 1.5, 6.0, ((0, 4), (1, 8)))
    up_pre = gaussian(arg_keys[2], (TOKENS, FF), 1.0, 6.0, ((0, 4), (1, 8)))
    hidden_grad = gaussian(arg_keys[3], (TOKENS, FF), 0.1, 0.59765625, ((0, 4), (1, 8)))
    gate_blocks = gaussian(arg_keys[4], (N_WT * MAXB, BLK, BLK), (D // 4) ** -0.5, 0.125, ((0, 8),))
    up_blocks = gaussian(arg_keys[5], (N_WT * MAXB, BLK, BLK), (D // 4) ** -0.5, 0.125, ((0, 8),))
    block_rows = draw_block_rows(jax.random.fold_in(arg_keys[9], 71), 0)
    block_cols = draw_block_cols(jax.random.fold_in(arg_keys[9], 71), 0)
    block_count = draw_block_count(jax.random.fold_in(arg_keys[9], 71), 0)
    return dict(activations=activations, gate_pre=gate_pre, up_pre=up_pre, hidden_grad=hidden_grad, gate_blocks=gate_blocks, up_blocks=up_blocks, block_rows=block_rows, block_cols=block_cols, block_count=block_count)


def reference(activations, gate_pre, up_pre, hidden_grad, gate_blocks, up_blocks, block_rows, block_cols, block_count):
    gate_value = gate_pre.astype(jnp.float32)
    up_value = up_pre.astype(jnp.float32)
    grad_value = hidden_grad.astype(jnp.float32)
    sigmoid_gate = jax.nn.sigmoid(gate_value)
    gate_grad = (grad_value * up_value * sigmoid_gate * (1.0 + gate_value * (1.0 - sigmoid_gate))).astype(jnp.bfloat16)
    up_grad = (grad_value * gate_value * sigmoid_gate).astype(jnp.bfloat16)
    token_count = activations.shape[0]
    gate_cols = gate_grad.reshape(token_count, FBLK, BLK)
    up_cols = up_grad.reshape(token_count, FBLK, BLK)
    feature_cols = activations.reshape(token_count, DBLK, BLK)
    slot_index = jnp.arange(N_WT * MAXB, dtype=jnp.int32) % MAXB
    alive = (slot_index < jnp.repeat(block_count, MAXB)).reshape(N_WT, MAXB)
    rows = block_rows.reshape(N_WT, MAXB)
    cols = block_cols.reshape(N_WT, MAXB)
    gate_w = gate_blocks.reshape(N_WT, MAXB, BLK, BLK)
    up_w = up_blocks.reshape(N_WT, MAXB, BLK, BLK)

    def owner(carry, inputs):
        rows_w, cols_w, alive_w, gate_ww, up_ww = inputs
        mask = alive_w[:, None, None]
        gate_m = jnp.where(mask, gate_ww.astype(jnp.float32), jnp.float32(0.0))
        up_m = jnp.where(mask, up_ww.astype(jnp.float32), jnp.float32(0.0))
        gate_sel = jnp.take(gate_cols, rows_w, axis=1).astype(jnp.float32)
        up_sel = jnp.take(up_cols, rows_w, axis=1).astype(jnp.float32)
        contrib = jnp.einsum('tsj,sjk->tsk', gate_sel, gate_m) + jnp.einsum('tsj,sjk->tsk', up_sel, up_m)
        summed = jax.ops.segment_sum(jnp.transpose(contrib, (1, 0, 2)), cols_w, num_segments=DBLK)
        feature_sel = jnp.take(feature_cols, cols_w, axis=1).astype(jnp.float32)
        results = []
        for chosen in (gate_sel, up_sel):
            total = jnp.zeros((MAXB, BLK, BLK), jnp.float32)
            for group in range(N_TOK):
                lower = group * TOK_DEV
                upper = lower + TOK_DEV
                partial_sum = jnp.einsum('tsj,tsk->sjk', chosen[lower:upper], feature_sel[lower:upper])
                rounded = lax.optimization_barrier(partial_sum.astype(jnp.bfloat16))
                total = total + rounded.astype(jnp.float32)
            results.append(jnp.where(mask, total, jnp.float32(0.0)).astype(jnp.bfloat16))
        return carry + summed, (results[0], results[1])

    start = jnp.zeros((DBLK, token_count, BLK), jnp.float32)
    total_grad, grads = lax.scan(owner, start, (rows, cols, alive, gate_w, up_w))
    input_grad = jnp.transpose(total_grad, (1, 0, 2)).reshape(token_count, DBLK * BLK).astype(jnp.bfloat16)
    gate_weight_grad = grads[0].reshape(N_WT * MAXB, BLK, BLK)
    up_weight_grad = grads[1].reshape(N_WT * MAXB, BLK, BLK)
    return (input_grad, gate_weight_grad, up_weight_grad)
```

```python
import functools

import jax
import jax.numpy as jnp
from jax import lax
from jax.experimental import pallas as pl
from jax.experimental.pallas import tpu as pltpu
from jax.sharding import PartitionSpec as P

F32 = jnp.float32
BF16 = jnp.bfloat16
VMEM_LIMIT = 56 * 1024 * 1024


def act_kernel(g_ref, u_ref, h_ref, gu_ref, gut_ref):
    g = g_ref[...].astype(F32)
    u = u_ref[...].astype(F32)
    h = h_ref[...].astype(F32)
    sig = jax.nn.sigmoid(g)
    gate = (h * u * sig * (1.0 + g * (1.0 - sig))).astype(BF16)
    up = (h * g * sig).astype(BF16)
    width = gate.shape[1]
    gu_ref[0, :, :width] = gate
    gu_ref[0, :, width:] = up
    gut_ref[0, :width, :] = gate.T
    gut_ref[0, width:, :] = up.T


def hidden_grads(gate_pre, up_pre, hidden_grad, width):
    toks, hidden = gate_pre.shape
    owned = hidden // width
    spec = pl.BlockSpec((toks, width), lambda r: (0, r))
    return pl.pallas_call(
        act_kernel,
        grid=(owned,),
        in_specs=[spec] * 3,
        out_specs=[
            pl.BlockSpec((1, toks, 2 * width), lambda r: (r, 0, 0)),
            pl.BlockSpec((1, 2 * width, toks), lambda r: (r, 0, 0)),
        ],
        out_shape=[
            jax.ShapeDtypeStruct((owned, toks, 2 * width), BF16),
            jax.ShapeDtypeStruct((owned, 2 * width, toks), BF16),
        ],
        name="hidden_grads",
    )(gate_pre, up_pre, hidden_grad)


def dx_kernel(group, rows, cols, count, gu_ref, gw_ref, uw_ref, out_ref, acc):
    step = pl.program_id(0)
    first = step * group
    live = jnp.clip(count[0] - first, 0, group)
    width = gw_ref.shape[-1]
    per = out_ref.shape[2] // width

    @pl.when(step == 0)
    def _():
        acc[...] = jnp.zeros_like(acc)

    def one(j):
        w = jnp.concatenate([gw_ref[j], uw_ref[j]], axis=0)
        c = cols[first + j]
        acc[c] += jnp.dot(gu_ref[rows[first + j]], w, preferred_element_type=F32)

    @pl.when(live == group)
    def _():
        for j in range(group):
            one(j)

    @pl.when(live < group)
    def _():
        @pl.loop(0, live)
        def _(j):
            one(j)

    @pl.when(step == pl.num_programs(0) - 1)
    def _():
        @pl.loop(0, out_ref.shape[0])
        def _(i):
            for k in range(per):
                out_ref[i, :, k * width : (k + 1) * width] = acc[i * per + k].astype(BF16)


def input_terms(rows, cols, count, gu, gate_blocks, up_blocks, n_wt, feats):
    slots, width, _ = gate_blocks.shape
    owned, toks, _ = gu.shape
    group = 8
    wspec = pl.BlockSpec((group, width, width), lambda s, *_: (s, 0, 0))
    return pl.pallas_call(
        functools.partial(dx_kernel, group),
        grid_spec=pltpu.PrefetchScalarGridSpec(
            num_scalar_prefetch=3,
            grid=(slots // group,),
            in_specs=[
                pl.BlockSpec(gu.shape, lambda s, *_: (0, 0, 0), pipeline_mode=pl.Buffered(1)),
                wspec,
                wspec,
            ],
            out_specs=pl.BlockSpec(
                (n_wt, toks, feats), lambda s, *_: (0, 0, 0), pipeline_mode=pl.Buffered(1)
            ),
            scratch_shapes=[pltpu.VMEM((n_wt * feats // width, toks, width), F32)],
        ),
        out_shape=jax.ShapeDtypeStruct((n_wt, toks, feats), BF16),
        compiler_params=pltpu.CompilerParams(vmem_limit_bytes=VMEM_LIMIT),
        cost_estimate=pl.CostEstimate(
            flops=8 * slots * toks * width * width,
            bytes_accessed=4 * slots * width * width,
            transcendentals=0,
        ),
        name="input_terms",
    )(rows, cols, count, gu, gate_blocks, up_blocks)


def dw_kernel(group, rows, cols, count, gu0, gu1, a0, a1, gw_ref, uw_ref):
    first = pl.program_id(0) * group
    live = jnp.clip(count[0] - first, 0, group)
    width = gw_ref.shape[-1]
    per = a0.shape[2] // width

    def one(j):
        r = rows[first + j]
        c = cols[first + j]
        owner = lax.div(c, per)
        lanes = pl.ds(pl.multiple_of(lax.rem(c, per) * width, width), width)
        res = jnp.dot(gu0[r], a0[owner, :, lanes], preferred_element_type=F32)
        res = res + jnp.dot(gu1[r], a1[owner, :, lanes], preferred_element_type=F32)
        gw_ref[j] = res[:width].astype(BF16)
        uw_ref[j] = res[width:].astype(BF16)

    @pl.when(live == group)
    def _():
        for j in range(group):
            one(j)

    @pl.when(live < group)
    def _():
        gw_ref[...] = jnp.zeros_like(gw_ref)
        uw_ref[...] = jnp.zeros_like(uw_ref)

        @pl.loop(0, live)
        def _(j):
            one(j)


def weight_grads(rows, cols, count, gu0, gu1, a0, a1, slots, width):
    group = 8
    toks = a0.shape[1] + a1.shape[1]

    def whole(x):
        return pl.BlockSpec(x.shape, lambda s, *_: (0, 0, 0), pipeline_mode=pl.Buffered(1))

    ospec = pl.BlockSpec((group, width, width), lambda s, *_: (s, 0, 0))
    oshape = jax.ShapeDtypeStruct((slots, width, width), BF16)
    return pl.pallas_call(
        functools.partial(dw_kernel, group),
        grid_spec=pltpu.PrefetchScalarGridSpec(
            num_scalar_prefetch=3,
            grid=(slots // group,),
            in_specs=[whole(gu0), whole(gu1), whole(a0), whole(a1)],
            out_specs=[ospec, ospec],
        ),
        out_shape=[oshape, oshape],
        compiler_params=pltpu.CompilerParams(vmem_limit_bytes=VMEM_LIMIT),
        cost_estimate=pl.CostEstimate(
            flops=8 * slots * toks * width * width,
            bytes_accessed=4 * slots * width * width,
            transcendentals=0,
        ),
        name="weight_grads",
    )(rows, cols, count, gu0, gu1, a0, a1)


def body(
    n_tok,
    n_wt,
    activations,
    gate_pre,
    up_pre,
    hidden_grad,
    gate_blocks,
    up_blocks,
    block_rows,
    block_cols,
    block_count,
):
    slots, width, _ = gate_blocks.shape
    owned = gate_pre.shape[1] // width
    feats = activations.shape[1]
    rows = block_rows % owned
    far = [(t, t ^ 2) for t in range(n_tok)]
    near = [(t, t ^ 1) for t in range(n_tok)]

    a_pair = jnp.concatenate([activations, lax.ppermute(activations, "tok", far)], axis=0)
    a0 = lax.all_gather(a_pair, "wt", axis=0)
    gu, gut = hidden_grads(gate_pre, up_pre, hidden_grad, width)
    gu0 = jnp.concatenate([gut, lax.ppermute(gut, "tok", far)], axis=2)
    gu1 = lax.ppermute(gu0, "tok", near)
    terms = input_terms(rows, block_cols, block_count, gu, gate_blocks, up_blocks, n_wt, feats)
    input_grad = lax.psum_scatter(terms, "wt", scatter_dimension=0, tiled=False)
    a1 = lax.ppermute(a0, "tok", near)
    gate_weight_grad, up_weight_grad = weight_grads(
        rows, block_cols, block_count, gu0, gu1, a0, a1, slots, width
    )
    return (input_grad, gate_weight_grad, up_weight_grad)


def solution(mesh):
    in_specs = (
        P("tok", "wt"),
        P("tok", "wt"),
        P("tok", "wt"),
        P("tok", "wt"),
        P("wt", None, None),
        P("wt", None, None),
        P("wt"),
        P("wt"),
        P("wt"),
    )
    out_specs = (P("tok", "wt"), P("wt", None, None), P("wt", None, None))
    return jax.shard_map(
        functools.partial(body, mesh.shape["tok"], mesh.shape["wt"]),
        mesh=mesh,
        in_specs=in_specs,
        out_specs=out_specs,
        check_vma=False,
    )
```
